32 devices in a mesh: zn: 2 (over x), zw: 16 (over z, y, core).
Axes of the slice: x: 2, y: 2, z: 4, core: 2. Of those that a mesh axis runs over, the one named last changes fastest.
Arguments:
- basis: float32 [64, 32, 8, 256], P(None, 'zw', None, 'zn'), may hold values from -360 to 360
- coupling: bfloat16 [27, 32, 8, 256], P(None, 'zw', None, 'zn'), may hold values from -0.099609375 to 0.099609375
Outputs:
- q_basis: float32 [64, 32, 8, 256], P(None, 'zw', None, 'zn')
- r_factor: float32 [64, 64], replicated
The draws below stay inside these ranges and needn't reach their ends.
All inputs are finite; a program needn't handle non-finite values.
Results may differ from the reference program's by a relative error of at most 0.0003.
Values may be sent and summed in bfloat16 or wider, within the bound.
A program may use at most 64 MiB of HBM per device.

```python
import math
import jax
import jax.numpy as jnp
from jax import lax

K = 64
NX = 8
NY = 256
NZ = 32


def draw_basis(key, part):
    key = jax.random.fold_in(key, 11)
    key_base = jax.random.fold_in(key, 0)
    key_cell = jax.random.fold_in(key, 1)
    key_column = jax.random.fold_in(key, 2)
    key_paired = jax.random.fold_in(key, 4)
    full_shape = (K, NZ, NX, NY)
    depth_z = jnp.arange(NZ, dtype=jnp.float32) / max(NZ - 1, 1)
    depth_y = jnp.arange(NY, dtype=jnp.float32) / max(NY - 1, 1)
    profile = ((1.0 + 2.0 * depth_z)[:, None, None] * (1.0 + 2.0 * depth_y)[None, None, :] / 3.0)[None]
    cell_scale = jnp.exp(jax.random.uniform(key_cell, (1, NZ, NX, NY), jnp.float32, 0.0, math.log(3.0)))
    column_scale = jnp.exp(jax.random.uniform(key_column, (K, 1, 1, 1), jnp.float32, 0.0, math.log(10.0)))
    innovation = jnp.clip(jax.random.normal(key_base, full_shape, jnp.float32), -3.0, 3.0) * 0.625
    paired = jax.random.randint(key_paired, (), 1, K, dtype=jnp.int32)

    def chain_step(previous, inputs):
        column_index, fresh_term = inputs
        nearby = previous + 0.03125 * fresh_term
        chained = 0.5 * previous + fresh_term
        mixed_value = jnp.where(column_index == paired, nearby, chained)
        return (mixed_value, mixed_value)
    leading = innovation[0]
    _, remaining = lax.scan(chain_step, leading, (jnp.arange(1, K, dtype=jnp.int32), innovation[1:]))
    values = jnp.concatenate([leading[None], remaining], axis=0)
    return (values * profile * cell_scale * column_scale).astype(jnp.float32)


def level_of(key, extent, pieces, low, largest):
    factor_of, own = 1.0, jax.random.fold_in(key, 6)
    for dim, blocks in pieces:
        heights = jnp.exp(jax.random.uniform(jax.random.fold_in(own, dim), (blocks,), jnp.float32, low / len(pieces), largest / len(pieces)))
        factor_of = factor_of * jnp.repeat(heights, extent[dim] // blocks).reshape([-1 if axis == dim else 1 for axis in range(len(extent))])
    return factor_of


def setup_inputs(seed: int = 0) -> dict:
    key_list = jax.random.split(jax.random.key(seed), 3)
    return {
        "basis": draw_basis(jax.random.fold_in(key_list[2], 71), 0),
        "coupling": jnp.clip(jax.random.uniform(key_list[1], (27, NZ, NX, NY), jnp.float32, -0.099609375, 0.099609375) * level_of(key_list[1], (27, NZ, NX, NY), ((1, 16), (3, 2)), -0.4, 0.0), -0.099609375, 0.099609375).astype(jnp.bfloat16),
    }


def sweep(extended, coupling):
    planes_here = coupling.shape[1]
    summed = extended[1:planes_here + 1]
    for shift_z in (-1, 0, 1):
        source = extended[1 + shift_z:1 + shift_z + planes_here]
        for shift_x in (-1, 0, 1):
            for shift_y in (-1, 0, 1):
                offset = 9 * (shift_z + 1) + 3 * (shift_x + 1) + shift_y + 1
                rolled = jnp.roll(source, (-shift_x, -shift_y), axis=(1, 2))
                summed = summed + coupling[offset].astype(jnp.float32) * rolled
    return summed

def propagate(column, coupling):
    field_now = column
    for repeat in range(2):
        extended = jnp.pad(field_now, ((1, 1), (0, 0), (0, 0)))
        field_now = sweep(extended, coupling)
    return field_now

def upper_cholesky(gram_matrix):
    order = gram_matrix.shape[0]
    places = jnp.arange(order, dtype=jnp.int32)

    def one_row(index, upper):
        column = lax.dynamic_slice_in_dim(upper, index, 1, 1)[:, 0]
        target = lax.dynamic_slice_in_dim(gram_matrix, index, 1, 0)[0]
        remain = target - jnp.dot(column, upper, precision=lax.Precision.HIGHEST)
        pivot = jnp.sqrt(jnp.sum(jnp.where(places == index, remain, 0.0)))
        new_row = jnp.where(places > index, remain / pivot, jnp.where(places == index, pivot, 0.0))
        return lax.dynamic_update_slice_in_dim(upper, new_row[None].astype(upper.dtype), index, 0)
    return lax.fori_loop(0, order, one_row, jnp.zeros_like(gram_matrix))

def upper_inverse(upper):
    order = upper.shape[0]
    places = jnp.arange(order, dtype=jnp.int32)

    def one_row(step, inverse):
        index = order - 1 - step
        row = lax.dynamic_slice_in_dim(upper, index, 1, 0)[0]
        pivot = jnp.sum(jnp.where(places == index, row, 0.0))
        above = jnp.where(places > index, row, 0.0)
        unit = jnp.where(places == index, 1.0, 0.0).astype(upper.dtype)
        new_row = (unit - jnp.dot(above, inverse, precision=lax.Precision.HIGHEST)) / pivot
        return lax.dynamic_update_slice_in_dim(inverse, new_row[None].astype(upper.dtype), index, 0)
    return lax.fori_loop(0, order, one_row, jnp.zeros_like(upper))

def reference(basis, coupling):
    field_now = lax.map(lambda column: propagate(column, coupling), basis)
    columns = field_now.shape[0]
    flat_basis = field_now.reshape(columns, -1)
    total_cells = flat_basis.shape[1]
    gram_matrix = jnp.dot(flat_basis, flat_basis.T, precision=lax.Precision.HIGHEST)
    upper_factor = upper_cholesky(gram_matrix)
    inverse = upper_inverse(upper_factor)
    q_flat = jnp.dot(inverse.T, flat_basis, precision=lax.Precision.HIGHEST)
    scale_root = jnp.sqrt(jnp.float32(total_cells))
    q_basis = (q_flat * scale_root).reshape(field_now.shape)
    return (q_basis, upper_factor / scale_root)
```

```python
import functools

import jax
import jax.numpy as jnp
from jax import lax
from jax.experimental import pallas as pl
from jax.experimental.pallas import tpu as pltpu
from jax.sharding import PartitionSpec as P

MESH = pl.DeviceIdType.MESH
CHUNKS = 4


def inner_size(n):
    s = 1
    while s * s < n:
        s *= 2
    while n % s:
        s //= 2
    return s


def kernel(
    n_zn, n_zw, cells, basis, coupling, q_out, r_out,
    f0, f1, x2, cpl, ysend, yrecv, xs, buf_a, buf_b,
    load_sem, z_send, z_recv, y_send, y_recv, a_send, a_recv, b_send, b_recv,
):
    zn = lax.axis_index("zn")
    zw = lax.axis_index("zw")
    has_lo = zw > 0
    has_hi = zw < n_zw - 1
    cols = basis.shape[0]
    per = cols // CHUNKS
    n_dir = yrecv.shape[0]
    si = inner_size(n_zw)
    so = n_zw // si
    n_a = n_zn * si
    sides = (1,) if n_dir == 1 else (1, n_zn - 1)

    def beside(step):
        return (zn + step) % n_zn

    inner = zw % si
    outer = zw // si
    me_a = zn * si + inner

    def partner_a(off):
        other = (me_a + off) % n_a
        return other, {"zn": other // si, "zw": outer * si + other % si}

    def partner_b(off):
        other = (outer + off) % so
        return other, {"zn": zn, "zw": other * si + inner}

    barrier = pltpu.get_barrier_semaphore()

    def greet(dev):
        pl.semaphore_signal(barrier, inc=1, device_id=dev, device_id_type=MESH)

    for present, dz in ((has_lo, -1), (has_hi, 1)):
        @pl.when(present)
        def _(dz=dz):
            greet({"zn": zn, "zw": zw + dz})
            for side in sides:
                greet({"zn": beside(side), "zw": zw + dz})
    for off in range(1, n_a):
        greet(partner_a(off)[1])
    for off in range(1, so):
        greet(partner_b(off)[1])

    loads = [
        pltpu.make_async_copy(basis.at[:, z], f0.at[1 + z], load_sem.at[z]) for z in range(2)
    ]
    for copy in loads:
        copy.start()

    lane = lax.broadcasted_iota(jnp.int32, (8, 128), 1)
    sub = lax.broadcasted_iota(jnp.int32, (8, 128), 0)
    pair = lane // 2
    zero_tile = jnp.zeros((8, 128), jnp.float32)

    for present, plane in ((has_lo, 0), (has_hi, 3)):
        @pl.when(jnp.logical_not(present))
        def _(plane=plane):
            f0[plane] = jnp.zeros(f0.shape[1:], jnp.float32)
            f1[plane] = jnp.zeros(f1.shape[1:], jnp.float32)
            for d in range(n_dir):
                for c in range(CHUNKS + 1):
                    yrecv[d, c, plane] = zero_tile

    total = (n_a - 1) + (so - 1)
    both = has_lo.astype(jnp.int32) + has_hi.astype(jnp.int32)
    pl.semaphore_wait(barrier, total + both * (1 + len(sides)))

    def z_copy(e, c, way):
        part = pl.ds(c * per, per)
        if e == 0:
            src = basis.at[part, way]
        else:
            src = f1.at[1 + way, part]
        dst = (f0, f1)[e].at[3 if way == 0 else 0, part]
        return pltpu.make_async_remote_copy(
            src_ref=src, dst_ref=dst,
            send_sem=z_send.at[e, c, way], recv_sem=z_recv.at[e, c, way],
            device_id={"zn": zn, "zw": zw + (-1 if way == 0 else 1)}, device_id_type=MESH,
        )

    def z_start(e, c):
        for way, present in ((0, has_lo), (1, has_hi)):
            @pl.when(present)
            def _(way=way):
                z_copy(e, c, way).start()

    def z_wait(e, c):
        for way, present in ((0, has_hi), (1, has_lo)):
            @pl.when(present)
            def _(way=way):
                z_copy(e, c, way).wait_recv()

    def y_copy(slot, d, which):
        dz, src, dst = ((0, (0, 2), 1), (-1, (0, 1), 3), (1, (1, 1), 0))[which]
        return pltpu.make_async_remote_copy(
            src_ref=ysend.at[slot, pl.ds(src[0], src[1])],
            dst_ref=yrecv.at[d, slot, pl.ds(dst, src[1])],
            send_sem=y_send.at[slot, d, which], recv_sem=y_recv.at[slot, d, which],
            device_id={"zn": beside(sides[d]), "zw": zw + dz}, device_id_type=MESH,
        )

    def y_start(slot):
        for d in range(n_dir):
            y_copy(slot, d, 0).start()
            for which, present in ((1, has_lo), (2, has_hi)):
                @pl.when(present)
                def _(d=d, which=which):
                    y_copy(slot, d, which).start()

    def y_wait(slot):
        for d in range(n_dir):
            y_copy(slot, d, 0).wait_recv()
            for which, present in ((1, has_hi), (2, has_lo)):
                @pl.when(present)
                def _(d=d, which=which):
                    y_copy(slot, d, which).wait_recv()

    for c in range(CHUNKS):
        z_start(0, c)

    for copy in loads:
        copy.wait()

    def pack_into(packed, tile, k):
        return jnp.where(pair == k, pltpu.roll(tile, 2 * k + 1, 1), packed)

    def pack_first(step, packs):
        packs = list(packs)
        for u in range(4):
            k = step * 4 + u
            for z in range(2):
                packs[z] = pack_into(packs[z], f0[1 + z, k], k)
        return tuple(packs)

    packs = lax.fori_loop(0, cols // 4, pack_first, (zero_tile, zero_tile))
    for z in range(2):
        ysend[0, z] = packs[z]
    y_start(0)

    for z in range(2):
        for b in range(3):
            for a in range(3):
                for c in range(3):
                    tile = coupling[9 * a + 3 * b + c, z].astype(jnp.float32)
                    if b != 1:
                        tile = pltpu.roll(tile, (b - 1) % 8, 0)
                    cpl[z, 9 * b + 3 * a + c] = tile

    def arrived(slot):
        result = []
        for plane in range(4):
            tile = yrecv[0, slot, plane]
            if n_dir == 2:
                tile = jnp.where(lane % 2 == 0, tile, yrecv[1, slot, plane])
            result.append(tile)
        return result

    def step_column(f, k, edges):
        shifted = []
        for plane in range(4):
            tile = f[plane, k]
            edge = pltpu.roll(edges[plane], 127 - 2 * k, 1)
            before = pltpu.roll(jnp.where(lane == 127, edge, tile), 1, 1)
            after = pltpu.roll(jnp.where(lane == 0, edge, tile), 127, 1)
            shifted.append((before, tile, after))
        outs = []
        for z in range(2):
            out = shifted[z + 1][1]
            for b in range(3):
                acc = None
                for a in range(3):
                    for c in range(3):
                        term = cpl[z, 9 * b + 3 * a + c] * shifted[z + a][c]
                        acc = term if acc is None else acc + term
                if b != 1:
                    acc = pltpu.roll(acc, (1 - b) % 8, 0)
                out = out + acc
            outs.append(out)
        return outs

    y_wait(0)
    for c in range(CHUNKS):
        z_wait(0, c)
        edges = arrived(0)

        def first(step, packs, c=c, edges=edges):
            packs = list(packs)
            for u in range(2):
                k = c * per + step * 2 + u
                outs = step_column(f0, k, edges)
                for z in range(2):
                    f1[1 + z, k] = outs[z]
                    packs[z] = pack_into(packs[z], outs[z], k)
            return tuple(packs)

        packs = lax.fori_loop(0, per // 2, first, (zero_tile, zero_tile))
        for z in range(2):
            ysend[1 + c, z] = packs[z]
        y_start(1 + c)
        z_start(1, c)

    for c in range(CHUNKS):
        y_wait(1 + c)
        z_wait(1, c)
        edges = arrived(1 + c)

        def second(step, carry, c=c, edges=edges):
            for u in range(2):
                k = c * per + step * 2 + u
                outs = step_column(f1, k, edges)
                for z in range(2):
                    x2[z, pl.ds(pl.multiple_of(k * 8, 8), 8), :] = outs[z]
            return carry

        lax.fori_loop(0, per // 2, second, 0)

    for z in range(2):
        for x in range(8):
            piece = x2[z, pl.ds(x, cols, stride=8), :]
            at = (z * 8 + x) * 128
            high = piece.astype(jnp.bfloat16)
            rest = piece - high.astype(jnp.float32)
            mid = rest.astype(jnp.bfloat16)
            low = (rest - mid.astype(jnp.float32)).astype(jnp.bfloat16)
            xs[0:cols, at : at + 128] = high
            xs[cols : 2 * cols, at : at + 128] = mid
            xs[2 * cols : 3 * cols, at : at + 128] = low

    products = lax.dot_general(
        xs[...], xs[...], (((1,), (1,)), ((), ())), preferred_element_type=jnp.float32
    )
    rows = products[0:cols] + (products[cols : 2 * cols] + products[2 * cols :])
    gram = rows[:, 0:cols] + (rows[:, cols : 2 * cols] + rows[:, 2 * cols :])
    half = cols // 2
    packed = jnp.concatenate([gram[0:half], gram[half:]], axis=1)

    def exchange(buf, me, n, partner, send, recv, value):
        buf[me] = value
        copies = []
        for off in range(1, n):
            _, dev = partner(off)
            copy = pltpu.make_async_remote_copy(
                src_ref=buf.at[me], dst_ref=buf.at[me],
                send_sem=send.at[off], recv_sem=recv.at[me],
                device_id=dev, device_id_type=MESH,
            )
            copy.start()
            copies.append(copy)
        for off in range(1, n):
            other, dev = partner(off)
            pltpu.make_async_remote_copy(
                src_ref=buf.at[other], dst_ref=buf.at[other],
                send_sem=send.at[off], recv_sem=recv.at[other],
                device_id=dev, device_id_type=MESH,
            ).wait_recv()
        out = buf[0]
        for i in range(1, n):
            out = out + buf[i]
        return out, copies

    packed, sent_a = exchange(buf_a, me_a, n_a, partner_a, a_send, a_recv, packed)
    packed, sent_b = exchange(buf_b, outer, so, partner_b, b_send, b_recv, packed)

    blocks = cols // 8
    tiles = []
    for i in range(blocks):
        if i * 8 < half:
            tile = packed[i * 8 : i * 8 + 8]
        else:
            at = i * 8 - half
            tile = pltpu.roll(packed[at : at + 8], 64, 1)
        unit = jnp.where(lane - cols == sub + 8 * i, 1.0, 0.0)
        tiles.append(jnp.where(lane < cols, tile, unit))
    pivots = [zero_tile] * blocks
    for k in range(cols):
        own, r = k // 8, k % 8
        row = jnp.broadcast_to(tiles[own][r : r + 1, :], (8, 128))
        column = jnp.broadcast_to(tiles[own][:, k : k + 1], (8, 128))
        pivot = jnp.broadcast_to(column[r : r + 1, :], (8, 128))
        pivots[own] = jnp.where(sub == r, pivot, pivots[own])
        scaled = row * (1.0 / pivot)
        for i in range(own, blocks):
            if i > own:
                column = jnp.broadcast_to(tiles[i][:, k : k + 1], (8, 128))
            elif r == 7:
                continue
            else:
                column = jnp.where(sub > r, column, 0.0)
            tiles[i] = tiles[i] - column * scaled

    root = jnp.float32(cells) ** 0.5
    weights = []
    for i in range(blocks):
        scale = 1.0 / jnp.sqrt(pivots[i])
        tile = tiles[i] * scale
        upper = jnp.where(lane >= sub + 8 * i, tile, 0.0) / root
        r_out[8 * i : 8 * i + 8, :] = upper[:, 0:cols]
        weights.append(pltpu.roll(tile, 64, 1)[:, 0:cols] * root)
    weight = jnp.concatenate(weights, axis=0)
    high = weight.astype(jnp.bfloat16)
    rest = weight - high.astype(jnp.float32)
    mid = rest.astype(jnp.bfloat16)
    low = (rest - mid.astype(jnp.float32)).astype(jnp.bfloat16)
    stacked = jnp.concatenate([jnp.concatenate([w] * 3, axis=1) for w in (high, mid, low)], axis=0)
    for z in range(2):
        for x in range(0, 8, 2):
            at = (z * 8 + x) * 128
            got = jnp.dot(stacked, xs[:, at : at + 256], preferred_element_type=jnp.float32)
            got = got[0:cols] + (got[cols : 2 * cols] + got[2 * cols :])
            for u in range(2):
                x2[z, pl.ds(x + u, cols, stride=8), :] = got[:, u * 128 : u * 128 + 128]
    for z in range(2):
        q_out[:, z] = x2[z].reshape(cols, 8, 128)

    for e in range(2):
        for c in range(CHUNKS):
            for way, present in ((0, has_lo), (1, has_hi)):
                @pl.when(present)
                def _(e=e, c=c, way=way):
                    z_copy(e, c, way).wait_send()
    for slot in range(CHUNKS + 1):
        for d in range(n_dir):
            y_copy(slot, d, 0).wait_send()
            for which, present in ((1, has_lo), (2, has_hi)):
                @pl.when(present)
                def _(slot=slot, d=d, which=which):
                    y_copy(slot, d, which).wait_send()
    for copy in sent_a + sent_b:
        copy.wait_send()


def solution(mesh):
    n_zn, n_zw = mesh.shape["zn"], mesh.shape["zw"]

    def on_device(basis, coupling):
        cols, planes, nx, span = basis.shape
        si = inner_size(n_zw)
        so = n_zw // si
        n_a = n_zn * si
        n_dir = 1 if n_zn == 2 else 2
        f32 = jnp.float32
        dma = pltpu.SemaphoreType.DMA
        cells = planes * nx * span * n_zn * n_zw
        return pl.pallas_call(
            functools.partial(kernel, n_zn, n_zw, cells),
            out_shape=(
                jax.ShapeDtypeStruct(basis.shape, f32),
                jax.ShapeDtypeStruct((cols, cols), f32),
            ),
            in_specs=[pl.BlockSpec(memory_space=pl.ANY), pl.BlockSpec(memory_space=pltpu.VMEM)],
            out_specs=(
                pl.BlockSpec(memory_space=pltpu.VMEM),
                pl.BlockSpec(memory_space=pltpu.VMEM),
            ),
            scratch_shapes=[
                pltpu.VMEM((4, cols, nx, span), f32),
                pltpu.VMEM((4, cols, nx, span), f32),
                pltpu.VMEM((planes, cols * nx, span), f32),
                pltpu.VMEM((planes, 27, nx, span), f32),
                pltpu.VMEM((CHUNKS + 1, 2, nx, span), f32),
                pltpu.VMEM((n_dir, CHUNKS + 1, 4, nx, span), f32),
                pltpu.VMEM((3 * cols, planes * nx * span), jnp.bfloat16),
                pltpu.VMEM((n_a, cols // 2, 2 * cols), f32),
                pltpu.VMEM((so, cols // 2, 2 * cols), f32),
                dma((2,)),
                dma((2, CHUNKS, 2)),
                dma((2, CHUNKS, 2)),
                dma((CHUNKS + 1, n_dir, 3)),
                dma((CHUNKS + 1, n_dir, 3)),
                dma((n_a,)),
                dma((n_a,)),
                dma((so,)),
                dma((so,)),
            ],
            compiler_params=pltpu.CompilerParams(
                collective_id=0, has_side_effects=True, vmem_limit_bytes=32 * 1024 * 1024
            ),
        )(basis, coupling)

    spec = P(None, "zw", None, "zn")
    return jax.shard_map(
        on_device, mesh=mesh, in_specs=(spec, spec), out_specs=(spec, P()), check_vma=False
    )
```

```python
import functools

import jax
import jax.numpy as jnp
from jax import lax
from jax.experimental import pallas as pl
from jax.experimental.pallas import tpu as pltpu
from jax.sharding import PartitionSpec as P

MESH = pl.DeviceIdType.MESH
CHUNKS = 4


def inner_size(n):
    s = 1
    while s * s < n:
        s *= 2
    while n % s:
        s //= 2
    return s


def kernel(
    n_zn, n_zw, cells, basis, coupling, q_out, r_out,
    f0, f1, x2, cpl, ysend, yrecv, xs, buf_a, buf_b,
    load_sem, z_send, z_recv, y_send, y_recv, a_send, a_recv, b_send, b_recv,
):
    zn = lax.axis_index("zn")
    zw = lax.axis_index("zw")
    has_lo = zw > 0
    has_hi = zw < n_zw - 1
    cols = basis.shape[0]
    per = cols // CHUNKS
    n_dir = yrecv.shape[0]
    si = inner_size(n_zw)
    so = n_zw // si
    n_a = n_zn * si
    sides = (1,) if n_dir == 1 else (1, n_zn - 1)

    def beside(step):
        return (zn + step) % n_zn

    inner = zw % si
    outer = zw // si
    me_a = zn * si + inner

    def partner_a(off):
        other = (me_a + off) % n_a
        return other, {"zn": other // si, "zw": outer * si + other % si}

    def partner_b(off):
        other = (outer + off) % so
        return other, {"zn": zn, "zw": other * si + inner}

    barrier = pltpu.get_barrier_semaphore()

    def greet(dev):
        pl.semaphore_signal(barrier, inc=1, device_id=dev, device_id_type=MESH)

    for present, dz in ((has_lo, -1), (has_hi, 1)):
        @pl.when(present)
        def _(dz=dz):
            greet({"zn": zn, "zw": zw + dz})
            for side in sides:
                greet({"zn": beside(side), "zw": zw + dz})
    for off in range(1, n_a):
        greet(partner_a(off)[1])
    for off in range(1, so):
        greet(partner_b(off)[1])

    loads = [
        pltpu.make_async_copy(basis.at[:, z], f0.at[1 + z], load_sem.at[z]) for z in range(2)
    ]
    for copy in loads:
        copy.start()

    lane = lax.broadcasted_iota(jnp.int32, (8, 128), 1)
    sub = lax.broadcasted_iota(jnp.int32, (8, 128), 0)
    pair = lane // 2
    zero_tile = jnp.zeros((8, 128), jnp.float32)

    for present, plane in ((has_lo, 0), (has_hi, 3)):
        @pl.when(jnp.logical_not(present))
        def _(plane=plane):
            f0[plane] = jnp.zeros(f0.shape[1:], jnp.float32)
            f1[plane] = jnp.zeros(f1.shape[1:], jnp.float32)
            for d in range(n_dir):
                for e in range(2):
                    yrecv[d, e, plane] = jnp.zeros(yrecv.shape[3:], jnp.float32)

    total = (n_a - 1) + (so - 1)
    both = has_lo.astype(jnp.int32) + has_hi.astype(jnp.int32)
    pl.semaphore_wait(barrier, total + both * (1 + len(sides)))

    def z_copy(e, c, way):
        part = pl.ds(c * per, per)
        if e == 0:
            src = basis.at[part, way]
        else:
            src = f1.at[1 + way, part]
        dst = (f0, f1)[e].at[3 if way == 0 else 0, part]
        return pltpu.make_async_remote_copy(
            src_ref=src, dst_ref=dst,
            send_sem=z_send.at[e, c, way], recv_sem=z_recv.at[e, c, way],
            device_id={"zn": zn, "zw": zw + (-1 if way == 0 else 1)}, device_id_type=MESH,
        )

    def z_start(e, c):
        for way, present in ((0, has_lo), (1, has_hi)):
            @pl.when(present)
            def _(way=way):
                z_copy(e, c, way).start()

    def z_wait(e, c):
        for way, present in ((0, has_hi), (1, has_lo)):
            @pl.when(present)
            def _(way=way):
                z_copy(e, c, way).wait_recv()

    def y_copy(e, c, d, which):
        dz, src, dst = ((0, (0, 2), 1), (-1, (0, 1), 3), (1, (1, 1), 0))[which]
        if c is None:
            part, at = slice(None), CHUNKS
        else:
            part, at = pl.ds(c, 1), c
        return pltpu.make_async_remote_copy(
            src_ref=ysend.at[e, pl.ds(src[0], src[1]), part],
            dst_ref=yrecv.at[d, e, pl.ds(dst, src[1]), part],
            send_sem=y_send.at[at, d, which], recv_sem=y_recv.at[at, d, which],
            device_id={"zn": beside(sides[d]), "zw": zw + dz}, device_id_type=MESH,
        )

    def y_start(e, c):
        for d in range(n_dir):
            y_copy(e, c, d, 0).start()
            for which, present in ((1, has_lo), (2, has_hi)):
                @pl.when(present)
                def _(d=d, which=which):
                    y_copy(e, c, d, which).start()

    def y_wait(e, c):
        for d in range(n_dir):
            y_copy(e, c, d, 0).wait_recv()
            for which, present in ((1, has_hi), (2, has_lo)):
                @pl.when(present)
                def _(d=d, which=which):
                    y_copy(e, c, d, which).wait_recv()

    for c in range(CHUNKS):
        z_start(0, c)

    for copy in loads:
        copy.wait()

    def pack_into(packed, tile, u):
        return jnp.where(pair == u, pltpu.roll(tile, 2 * u + 1, 1), packed)

    def pack_first(c, carry):
        packs = [zero_tile, zero_tile]
        for u in range(per):
            for z in range(2):
                packs[z] = pack_into(packs[z], f0[1 + z, c * per + u], u)
        for z in range(2):
            ysend[0, z, c] = packs[z]
        return carry

    lax.fori_loop(0, CHUNKS, pack_first, 0)
    y_start(0, None)

    for z in range(2):
        for b in range(3):
            for a in range(3):
                for c in range(3):
                    tile = coupling[9 * a + 3 * b + c, z].astype(jnp.float32)
                    if b != 1:
                        tile = pltpu.roll(tile, (b - 1) % 8, 0)
                    cpl[z, 9 * b + 3 * a + c] = tile

    def arrived(e, c):
        result = []
        for plane in range(4):
            tile = yrecv[0, e, plane, c]
            if n_dir == 2:
                tile = jnp.where(lane % 2 == 0, tile, yrecv[1, e, plane, c])
            result.append(tile)
        return result

    def step_column(f, k, u, edges):
        shifted = []
        for plane in range(4):
            tile = f[plane, k]
            edge = pltpu.roll(edges[plane], 127 - 2 * u, 1)
            before = pltpu.roll(jnp.where(lane == 127, edge, tile), 1, 1)
            after = pltpu.roll(jnp.where(lane == 0, edge, tile), 127, 1)
            shifted.append((before, tile, after))
        outs = []
        for z in range(2):
            out = shifted[z + 1][1]
            for b in range(3):
                acc = None
                for a in range(3):
                    for c in range(3):
                        term = cpl[z, 9 * b + 3 * a + c] * shifted[z + a][c]
                        acc = term if acc is None else acc + term
                if b != 1:
                    acc = pltpu.roll(acc, (1 - b) % 8, 0)
                out = out + acc
            outs.append(out)
        return outs

    def first(c, carry):
        z_wait(0, c)
        edges = arrived(0, c)
        packs = [zero_tile, zero_tile]
        for u in range(per):
            k = c * per + u
            outs = step_column(f0, k, u, edges)
            for z in range(2):
                f1[1 + z, k] = outs[z]
                packs[z] = pack_into(packs[z], outs[z], u)
        for z in range(2):
            ysend[1, z, c] = packs[z]
        z_start(1, c)
        y_start(1, c)
        return carry

    def second(c, carry):
        y_wait(1, c)
        z_wait(1, c)
        edges = arrived(1, c)
        for u in range(per):
            k = c * per + u
            outs = step_column(f1, k, u, edges)
            for z in range(2):
                x2[z, pl.ds(pl.multiple_of(k * 8, 8), 8), :] = outs[z]
        return carry

    y_wait(0, None)
    lax.fori_loop(0, CHUNKS, first, 0)
    lax.fori_loop(0, CHUNKS, second, 0)

    for z in range(2):
        for x in range(8):
            piece = x2[z, pl.ds(x, cols, stride=8), :]
            at = (z * 8 + x) * 128
            high = piece.astype(jnp.bfloat16)
            rest = piece - high.astype(jnp.float32)
            mid = rest.astype(jnp.bfloat16)
            low = (rest - mid.astype(jnp.float32)).astype(jnp.bfloat16)
            xs[0:cols, at : at + 128] = high
            xs[cols : 2 * cols, at : at + 128] = mid
            xs[2 * cols : 3 * cols, at : at + 128] = low

    products = lax.dot_general(
        xs[...], xs[...], (((1,), (1,)), ((), ())), preferred_element_type=jnp.float32
    )
    rows = products[0:cols] + (products[cols : 2 * cols] + products[2 * cols :])
    gram = rows[:, 0:cols] + (rows[:, cols : 2 * cols] + rows[:, 2 * cols :])
    half = cols // 2
    packed = jnp.concatenate([gram[0:half], gram[half:]], axis=1)

    def exchange(buf, me, n, partner, send, recv, value):
        buf[me] = value
        copies = []
        for off in range(1, n):
            _, dev = partner(off)
            copy = pltpu.make_async_remote_copy(
                src_ref=buf.at[me], dst_ref=buf.at[me],
                send_sem=send.at[off], recv_sem=recv.at[me],
                device_id=dev, device_id_type=MESH,
            )
            copy.start()
            copies.append(copy)
        for off in range(1, n):
            other, dev = partner(off)
            pltpu.make_async_remote_copy(
                src_ref=buf.at[other], dst_ref=buf.at[other],
                send_sem=send.at[off], recv_sem=recv.at[other],
                device_id=dev, device_id_type=MESH,
            ).wait_recv()
        out = buf[0]
        for i in range(1, n):
            out = out + buf[i]
        return out, copies

    packed, sent_a = exchange(buf_a, me_a, n_a, partner_a, a_send, a_recv, packed)
    packed, sent_b = exchange(buf_b, outer, so, partner_b, b_send, b_recv, packed)

    blocks = cols // 8
    tiles = []
    for i in range(blocks):
        if i * 8 < half:
            tile = packed[i * 8 : i * 8 + 8]
        else:
            at = i * 8 - half
            tile = pltpu.roll(packed[at : at + 8], 64, 1)
        unit = jnp.where(lane - cols == sub + 8 * i, 1.0, 0.0)
        tiles.append(jnp.where(lane < cols, tile, unit))
    sums = [zero_tile] * blocks
    pivots = []
    for own in range(blocks):
        base = own * 8
        now = [tiles[i] - sums[i] for i in range(own, blocks)]
        columns = [
            [jnp.broadcast_to(tile[:, base + s : base + s + 1], (8, 128)) for s in range(8)]
            for tile in now
        ]
        block = [
            [jnp.broadcast_to(columns[0][s][t : t + 1, :], (8, 128)) for s in range(8)]
            for t in range(8)
        ]
        rows = [jnp.broadcast_to(now[0][s : s + 1, :], (8, 128)) for s in range(8)]
        done, pivot_tile = zero_tile, zero_tile
        add_block, add_rows = {}, {}
        add_columns = [dict() for _ in now]

        def plus(table, key, value):
            table[key] = table[key] + value if key in table else value

        def less(table, key, value):
            return value - table[key] if key in table else value

        for s in range(8):
            pivot = less(add_block, (s, s), block[s][s])
            inverse = 1.0 / pivot
            row = less(add_rows, s, rows[s])
            scaled = row * inverse
            done = jnp.where(sub == s, row, done)
            pivot_tile = jnp.where(sub == s, pivot, pivot_tile)
            entries = {t: less(add_block, (s, t), block[s][t]) for t in range(s + 1, 8)}
            factors = {t: entries[t] * inverse for t in entries}
            for t in entries:
                for v in range(t, 8):
                    plus(add_block, (t, v), entries[t] * factors[v])
                plus(add_rows, t, entries[t] * scaled)
            for j in range(1, len(now)):
                column = less(add_columns[j], s, columns[j][s])
                for t in entries:
                    plus(add_columns[j], t, column * factors[t])
                sums[own + j] = sums[own + j] + column * scaled
        tiles[own] = done
        pivots.append(pivot_tile)

    root = jnp.float32(cells) ** 0.5
    weights = []
    for i in range(blocks):
        scale = 1.0 / jnp.sqrt(pivots[i])
        tile = tiles[i] * scale
        upper = jnp.where(lane >= sub + 8 * i, tile, 0.0) / root
        r_out[8 * i : 8 * i + 8, :] = upper[:, 0:cols]
        weights.append(pltpu.roll(tile, 64, 1)[:, 0:cols] * root)
    weight = jnp.concatenate(weights, axis=0)
    high = weight.astype(jnp.bfloat16)
    rest = weight - high.astype(jnp.float32)
    mid = rest.astype(jnp.bfloat16)
    low = (rest - mid.astype(jnp.float32)).astype(jnp.bfloat16)
    stacked = jnp.concatenate([jnp.concatenate([w] * 3, axis=1) for w in (high, mid, low)], axis=0)
    for z in range(2):
        for x in range(0, 8, 2):
            at = (z * 8 + x) * 128
            got = jnp.dot(stacked, xs[:, at : at + 256], preferred_element_type=jnp.float32)
            got = got[0:cols] + (got[cols : 2 * cols] + got[2 * cols :])
            for u in range(2):
                x2[z, pl.ds(x + u, cols, stride=8), :] = got[:, u * 128 : u * 128 + 128]
    for z in range(2):
        q_out[:, z] = x2[z].reshape(cols, 8, 128)

    for e in range(2):
        for c in range(CHUNKS):
            for way, present in ((0, has_lo), (1, has_hi)):
                @pl.when(present)
                def _(e=e, c=c, way=way):
                    z_copy(e, c, way).wait_send()
    for e, c in [(0, None)] + [(1, c) for c in range(CHUNKS)]:
        for d in range(n_dir):
            y_copy(e, c, d, 0).wait_send()
            for which, present in ((1, has_lo), (2, has_hi)):
                @pl.when(present)
                def _(e=e, c=c, d=d, which=which):
                    y_copy(e, c, d, which).wait_send()
    for copy in sent_a + sent_b:
        copy.wait_send()


def solution(mesh):
    n_zn, n_zw = mesh.shape["zn"], mesh.shape["zw"]

    def on_device(basis, coupling):
        cols, planes, nx, span = basis.shape
        si = inner_size(n_zw)
        so = n_zw // si
        n_a = n_zn * si
        n_dir = 1 if n_zn == 2 else 2
        f32 = jnp.float32
        dma = pltpu.SemaphoreType.DMA
        cells = planes * nx * span * n_zn * n_zw
        return pl.pallas_call(
            functools.partial(kernel, n_zn, n_zw, cells),
            out_shape=(
                jax.ShapeDtypeStruct(basis.shape, f32),
                jax.ShapeDtypeStruct((cols, cols), f32),
            ),
            in_specs=[pl.BlockSpec(memory_space=pl.ANY), pl.BlockSpec(memory_space=pltpu.VMEM)],
            out_specs=(
                pl.BlockSpec(memory_space=pltpu.VMEM),
                pl.BlockSpec(memory_space=pltpu.VMEM),
            ),
            scratch_shapes=[
                pltpu.VMEM((4, cols, nx, span), f32),
                pltpu.VMEM((4, cols, nx, span), f32),
                pltpu.VMEM((planes, cols * nx, span), f32),
                pltpu.VMEM((planes, 27, nx, span), f32),
                pltpu.VMEM((2, 2, CHUNKS, nx, span), f32),
                pltpu.VMEM((n_dir, 2, 4, CHUNKS, nx, span), f32),
                pltpu.VMEM((3 * cols, planes * nx * span), jnp.bfloat16),
                pltpu.VMEM((n_a, cols // 2, 2 * cols), f32),
                pltpu.VMEM((so, cols // 2, 2 * cols), f32),
                dma((2,)),
                dma((2, CHUNKS, 2)),
                dma((2, CHUNKS, 2)),
                dma((CHUNKS + 1, n_dir, 3)),
                dma((CHUNKS + 1, n_dir, 3)),
                dma((n_a,)),
                dma((n_a,)),
                dma((so,)),
                dma((so,)),
            ],
            compiler_params=pltpu.CompilerParams(
                collective_id=0, has_side_effects=True, vmem_limit_bytes=32 * 1024 * 1024
            ),
        )(basis, coupling)

    spec = P(None, "zw", None, "zn")
    return jax.shard_map(
        on_device, mesh=mesh, in_specs=(spec, spec), out_specs=(spec, P()), check_vma=False
    )
```

```python
import functools

import jax
import jax.numpy as jnp
from jax import lax
from jax.experimental import pallas as pl
from jax.experimental.pallas import tpu as pltpu
from jax.sharding import PartitionSpec as P

MESH = pl.DeviceIdType.MESH
CHUNKS = 8


def inner_size(n):
    s = 1
    while s * s < n:
        s *= 2
    while n % s:
        s //= 2
    return s


def kernel(
    n_zn, n_zw, cells, basis, coupling_far, q_out, r_out,
    coupling, f0, f1, x2, cpl, ysend, yrecv, xs, buf_a, buf_b,
    load_sem, z_send, z_recv, y_send, y_recv, a_send, a_recv, b_send, b_recv,
):
    zn = lax.axis_index("zn")
    zw = lax.axis_index("zw")
    has_lo = zw > 0
    has_hi = zw < n_zw - 1
    cols = basis.shape[0]
    per = cols // CHUNKS
    n_dir = yrecv.shape[0]
    si = inner_size(n_zw)
    so = n_zw // si
    n_a = n_zn * si
    sides = (1,) if n_dir == 1 else (1, n_zn - 1)

    def beside(step):
        return (zn + step) % n_zn

    inner = zw % si
    outer = zw // si
    me_a = zn * si + inner

    def partner_a(off):
        other = (me_a + off) % n_a
        return other, {"zn": other // si, "zw": outer * si + other % si}

    def partner_b(off):
        other = (outer + off) % so
        return other, {"zn": zn, "zw": other * si + inner}

    barrier = pltpu.get_barrier_semaphore()

    def greet(dev):
        pl.semaphore_signal(barrier, inc=1, device_id=dev, device_id_type=MESH)

    for present, dz in ((has_lo, -1), (has_hi, 1)):
        @pl.when(present)
        def _(dz=dz):
            greet({"zn": zn, "zw": zw + dz})
            for side in sides:
                greet({"zn": beside(side), "zw": zw + dz})
    for off in range(1, n_a):
        greet(partner_a(off)[1])
    for off in range(1, so):
        greet(partner_b(off)[1])

    loads = [
        pltpu.make_async_copy(basis.at[:, z], f0.at[1 + z], load_sem.at[z]) for z in range(2)
    ]
    load_coupling = pltpu.make_async_copy(coupling_far, coupling, load_sem.at[2])
    for copy in loads:
        copy.start()
    load_coupling.start()

    lane = lax.broadcasted_iota(jnp.int32, (8, 128), 1)
    sub = lax.broadcasted_iota(jnp.int32, (8, 128), 0)
    pair = lane // 2
    zero_tile = jnp.zeros((8, 128), jnp.float32)

    for present, plane in ((has_lo, 0), (has_hi, 3)):
        @pl.when(jnp.logical_not(present))
        def _(plane=plane):
            f0[plane] = jnp.zeros(f0.shape[1:], jnp.float32)
            f1[plane] = jnp.zeros(f1.shape[1:], jnp.float32)
            for d in range(n_dir):
                for e in range(2):
                    yrecv[d, e, plane] = jnp.zeros(yrecv.shape[3:], jnp.float32)

    total = (n_a - 1) + (so - 1)
    both = has_lo.astype(jnp.int32) + has_hi.astype(jnp.int32)
    pl.semaphore_wait(barrier, total + both * (1 + len(sides)))

    def z_copy(e, c, way):
        part = pl.ds(c * per, per)
        if e == 0:
            src = basis.at[part, way]
        else:
            src = f1.at[1 + way, part]
        dst = (f0, f1)[e].at[3 if way == 0 else 0, part]
        return pltpu.make_async_remote_copy(
            src_ref=src, dst_ref=dst,
            send_sem=z_send.at[e, c, way], recv_sem=z_recv.at[e, c, way],
            device_id={"zn": zn, "zw": zw + (-1 if way == 0 else 1)}, device_id_type=MESH,
        )

    def z_start(e, c):
        for way, present in ((0, has_lo), (1, has_hi)):
            @pl.when(present)
            def _(way=way):
                z_copy(e, c, way).start()

    def z_wait(e, c):
        for way, present in ((0, has_hi), (1, has_lo)):
            @pl.when(present)
            def _(way=way):
                z_copy(e, c, way).wait_recv()

    def y_copy(e, c, d, which):
        dz, src, dst = ((0, (0, 2), 1), (-1, (0, 1), 3), (1, (1, 1), 0))[which]
        if c is None:
            part, at = slice(None), CHUNKS
        else:
            part, at = pl.ds(c, 1), c
        return pltpu.make_async_remote_copy(
            src_ref=ysend.at[e, pl.ds(src[0], src[1]), part],
            dst_ref=yrecv.at[d, e, pl.ds(dst, src[1]), part],
            send_sem=y_send.at[at, d, which], recv_sem=y_recv.at[at, d, which],
            device_id={"zn": beside(sides[d]), "zw": zw + dz}, device_id_type=MESH,
        )

    def y_start(e, c):
        for d in range(n_dir):
            y_copy(e, c, d, 0).start()
            for which, present in ((1, has_lo), (2, has_hi)):
                @pl.when(present)
                def _(d=d, which=which):
                    y_copy(e, c, d, which).start()

    def y_wait(e, c):
        for d in range(n_dir):
            y_copy(e, c, d, 0).wait_recv()
            for which, present in ((1, has_hi), (2, has_lo)):
                @pl.when(present)
                def _(d=d, which=which):
                    y_copy(e, c, d, which).wait_recv()

    for c in range(CHUNKS // 2):
        z_start(0, c)

    for copy in loads:
        copy.wait()

    def pack_into(packed, tile, u):
        return jnp.where(pair == u, pltpu.roll(tile, 2 * u + 1, 1), packed)

    def pack_first(c, carry):
        packs = [zero_tile, zero_tile]
        for u in range(per):
            for z in range(2):
                packs[z] = pack_into(packs[z], f0[1 + z, c * per + u], u)
        for z in range(2):
            ysend[0, z, c] = packs[z]
        return carry

    lax.fori_loop(0, CHUNKS, pack_first, 0)
    y_start(0, None)
    for c in range(CHUNKS // 2, CHUNKS):
        z_start(0, c)

    load_coupling.wait()
    for z in range(2):
        for b in range(3):
            for a in range(3):
                for c in range(3):
                    tile = coupling[9 * a + 3 * b + c, z].astype(jnp.float32)
                    if b != 1:
                        tile = pltpu.roll(tile, (b - 1) % 8, 0)
                    cpl[z, 9 * b + 3 * a + c] = tile

    def arrived(e, c):
        result = []
        for plane in range(4):
            tile = yrecv[0, e, plane, c]
            if n_dir == 2:
                tile = jnp.where(lane % 2 == 0, tile, yrecv[1, e, plane, c])
            result.append(tile)
        return result

    def step_column(f, k, u, edges):
        shifted = []
        for plane in range(4):
            tile = f[plane, k]
            edge = pltpu.roll(edges[plane], 127 - 2 * u, 1)
            before = pltpu.roll(jnp.where(lane == 127, edge, tile), 1, 1)
            after = pltpu.roll(jnp.where(lane == 0, edge, tile), 127, 1)
            shifted.append((before, tile, after))
        outs = []
        for z in range(2):
            out = shifted[z + 1][1]
            for b in range(3):
                acc = None
                for a in range(3):
                    for c in range(3):
                        term = cpl[z, 9 * b + 3 * a + c] * shifted[z + a][c]
                        acc = term if acc is None else acc + term
                if b != 1:
                    acc = pltpu.roll(acc, (1 - b) % 8, 0)
                out = out + acc
            outs.append(out)
        return outs

    def first(c, carry):
        z_wait(0, c)
        edges = arrived(0, c)
        packs = [zero_tile, zero_tile]
        for u in range(per):
            k = c * per + u
            outs = step_column(f0, k, u, edges)
            for z in range(2):
                f1[1 + z, k] = outs[z]
                packs[z] = pack_into(packs[z], outs[z], u)
        for z in range(2):
            ysend[1, z, c] = packs[z]
        y_start(1, c)
        z_start(1, c)
        return carry

    def second(c, carry):
        y_wait(1, c)
        z_wait(1, c)
        edges = arrived(1, c)
        for u in range(per):
            k = c * per + u
            outs = step_column(f1, k, u, edges)
            for z in range(2):
                x2[z, pl.ds(pl.multiple_of(k * 8, 8), 8), :] = outs[z]
        return carry

    y_wait(0, None)
    lax.fori_loop(0, CHUNKS, first, 0)
    lax.fori_loop(0, CHUNKS, second, 0)

    for z in range(2):
        for x in range(8):
            piece = x2[z, pl.ds(x, cols, stride=8), :]
            at = (z * 8 + x) * 128
            high = piece.astype(jnp.bfloat16)
            rest = piece - high.astype(jnp.float32)
            mid = rest.astype(jnp.bfloat16)
            low = (rest - mid.astype(jnp.float32)).astype(jnp.bfloat16)
            xs[0:cols, at : at + 128] = high
            xs[cols : 2 * cols, at : at + 128] = mid
            xs[2 * cols : 3 * cols, at : at + 128] = low

    products = lax.dot_general(
        xs[...], xs[...], (((1,), (1,)), ((), ())), preferred_element_type=jnp.float32
    )
    rows = products[0:cols] + (products[cols : 2 * cols] + products[2 * cols :])
    gram = rows[:, 0:cols] + (rows[:, cols : 2 * cols] + rows[:, 2 * cols :])
    half = cols // 2
    packed = jnp.concatenate([gram[0:half], gram[half:]], axis=1)

    def exchange(buf, me, n, partner, send, recv, value):
        buf[me] = value
        copies = []
        for off in range(1, n):
            _, dev = partner(off)
            copy = pltpu.make_async_remote_copy(
                src_ref=buf.at[me], dst_ref=buf.at[me],
                send_sem=send.at[off], recv_sem=recv.at[me],
                device_id=dev, device_id_type=MESH,
            )
            copy.start()
            copies.append(copy)
        for off in range(1, n):
            other, dev = partner(off)
            pltpu.make_async_remote_copy(
                src_ref=buf.at[other], dst_ref=buf.at[other],
                send_sem=send.at[off], recv_sem=recv.at[other],
                device_id=dev, device_id_type=MESH,
            ).wait_recv()
        out = buf[0]
        for i in range(1, n):
            out = out + buf[i]
        return out, copies

    packed, sent_a = exchange(buf_a, me_a, n_a, partner_a, a_send, a_recv, packed)
    packed, sent_b = exchange(buf_b, outer, so, partner_b, b_send, b_recv, packed)

    blocks = cols // 8
    tiles = []
    for i in range(blocks):
        if i * 8 < half:
            tile = packed[i * 8 : i * 8 + 8]
        else:
            at = i * 8 - half
            tile = pltpu.roll(packed[at : at + 8], 64, 1)
        unit = jnp.where(lane - cols == sub + 8 * i, 1.0, 0.0)
        tiles.append(jnp.where(lane < cols, tile, unit))
    sums = [zero_tile] * blocks
    pivots = []
    for own in range(blocks):
        base = own * 8
        now = [tiles[i] - sums[i] for i in range(own, blocks)]
        columns = [
            [jnp.broadcast_to(tile[:, base + s : base + s + 1], (8, 128)) for s in range(8)]
            for tile in now
        ]
        block = [
            [jnp.broadcast_to(columns[0][s][t : t + 1, :], (8, 128)) for s in range(8)]
            for t in range(8)
        ]
        rows = [jnp.broadcast_to(now[0][s : s + 1, :], (8, 128)) for s in range(8)]
        done, pivot_tile = zero_tile, zero_tile
        add_block, add_rows = {}, {}
        add_columns = [dict() for _ in now]

        def plus(table, key, value):
            table[key] = table[key] + value if key in table else value

        def less(table, key, value):
            return value - table[key] if key in table else value

        for s in range(8):
            pivot = less(add_block, (s, s), block[s][s])
            inverse = 1.0 / pivot
            row = less(add_rows, s, rows[s])
            scaled = row * inverse
            done = jnp.where(sub == s, row, done)
            pivot_tile = jnp.where(sub == s, pivot, pivot_tile)
            entries = {t: less(add_block, (s, t), block[s][t]) for t in range(s + 1, 8)}
            factors = {t: entries[t] * inverse for t in entries}
            for t in entries:
                for v in range(t, 8):
                    plus(add_block, (t, v), entries[t] * factors[v])
                plus(add_rows, t, entries[t] * scaled)
            for j in range(1, len(now)):
                column = less(add_columns[j], s, columns[j][s])
                for t in entries:
                    plus(add_columns[j], t, column * factors[t])
                sums[own + j] = sums[own + j] + column * scaled
        tiles[own] = done
        pivots.append(pivot_tile)

    root = jnp.float32(cells) ** 0.5
    weights = []
    for i in range(blocks):
        scale = 1.0 / jnp.sqrt(pivots[i])
        tile = tiles[i] * scale
        upper = jnp.where(lane >= sub + 8 * i, tile, 0.0) / root
        r_out[8 * i : 8 * i + 8, :] = upper[:, 0:cols]
        weights.append(pltpu.roll(tile, 64, 1)[:, 0:cols] * root)
    weight = jnp.concatenate(weights, axis=0)
    high = weight.astype(jnp.bfloat16)
    rest = weight - high.astype(jnp.float32)
    mid = rest.astype(jnp.bfloat16)
    low = (rest - mid.astype(jnp.float32)).astype(jnp.bfloat16)
    stacked = jnp.concatenate([jnp.concatenate([w] * 3, axis=1) for w in (high, mid, low)], axis=0)
    for z in range(2):
        for x in range(0, 8, 2):
            at = (z * 8 + x) * 128
            got = jnp.dot(stacked, xs[:, at : at + 256], preferred_element_type=jnp.float32)
            got = got[0:cols] + (got[cols : 2 * cols] + got[2 * cols :])
            for u in range(2):
                x2[z, pl.ds(x + u, cols, stride=8), :] = got[:, u * 128 : u * 128 + 128]
    for z in range(2):
        q_out[:, z] = x2[z].reshape(cols, 8, 128)

    for e in range(2):
        for c in range(CHUNKS):
            for way, present in ((0, has_lo), (1, has_hi)):
                @pl.when(present)
                def _(e=e, c=c, way=way):
                    z_copy(e, c, way).wait_send()
    for e, c in [(0, None)] + [(1, c) for c in range(CHUNKS)]:
        for d in range(n_dir):
            y_copy(e, c, d, 0).wait_send()
            for which, present in ((1, has_lo), (2, has_hi)):
                @pl.when(present)
                def _(e=e, c=c, d=d, which=which):
                    y_copy(e, c, d, which).wait_send()
    for copy in sent_a + sent_b:
        copy.wait_send()


def solution(mesh):
    n_zn, n_zw = mesh.shape["zn"], mesh.shape["zw"]

    def on_device(basis, coupling):
        cols, planes, nx, span = basis.shape
        si = inner_size(n_zw)
        so = n_zw // si
        n_a = n_zn * si
        n_dir = 1 if n_zn == 2 else 2
        f32 = jnp.float32
        dma = pltpu.SemaphoreType.DMA
        cells = planes * nx * span * n_zn * n_zw
        return pl.pallas_call(
            functools.partial(kernel, n_zn, n_zw, cells),
            out_shape=(
                jax.ShapeDtypeStruct(basis.shape, f32),
                jax.ShapeDtypeStruct((cols, cols), f32),
            ),
            in_specs=[pl.BlockSpec(memory_space=pltpu.HBM)] * 2,
            out_specs=(
                pl.BlockSpec(memory_space=pltpu.VMEM),
                pl.BlockSpec(memory_space=pltpu.VMEM),
            ),
            scratch_shapes=[
                pltpu.VMEM(coupling.shape, coupling.dtype),
                pltpu.VMEM((4, cols, nx, span), f32),
                pltpu.VMEM((4, cols, nx, span), f32),
                pltpu.VMEM((planes, cols * nx, span), f32),
                pltpu.VMEM((planes, 27, nx, span), f32),
                pltpu.VMEM((2, 2, CHUNKS, nx, span), f32),
                pltpu.VMEM((n_dir, 2, 4, CHUNKS, nx, span), f32),
                pltpu.VMEM((3 * cols, planes * nx * span), jnp.bfloat16),
                pltpu.VMEM((n_a, cols // 2, 2 * cols), f32),
                pltpu.VMEM((so, cols // 2, 2 * cols), f32),
                dma((3,)),
                dma((2, CHUNKS, 2)),
                dma((2, CHUNKS, 2)),
                dma((CHUNKS + 1, n_dir, 3)),
                dma((CHUNKS + 1, n_dir, 3)),
                dma((n_a,)),
                dma((n_a,)),
                dma((so,)),
                dma((so,)),
            ],
            compiler_params=pltpu.CompilerParams(
                collective_id=0, has_side_effects=True, vmem_limit_bytes=32 * 1024 * 1024
            ),
        )(basis, coupling)

    spec = P(None, "zw", None, "zn")
    return jax.shard_map(
        on_device, mesh=mesh, in_specs=(spec, spec), out_specs=(spec, P()), check_vma=False
    )
```
